32 devices in a mesh: outer: 4 (over y, x), inner: 8 (over z, core).
Axes of the slice: x: 2, y: 2, z: 4, core: 2. Of those that a mesh axis runs over, the one named last changes fastest.
Arguments:
- shocks: float32 [32, 2, 60, 1024], P('outer', None, None, 'inner'), may hold values from -5 to 5, as said below
- node_rate: float32 [32, 2], P('outer'), may hold values from -0.025 to 0.06
- ladder_rung: int32 [32, 2], P('outer'), may hold values from 0 to 3
- cash_flows: float32 [60, 192], replicated, may hold values from 0.005 to 0.05
- owner_map: int32 [192], replicated, may hold values from 0 to 191, each once
- capital: float32 [32, 192], P('outer', 'inner'), may hold values from 0.3 to 1.5
Outputs:
- cohort_value: float32 [32, 2, 192], P('outer', None, 'inner')
- cohort_downside: float32 [32, 2, 192], P('outer', None, 'inner')
- fund_indexation: float32 [32, 2], P('outer')
- cohort_summary: float32 [2, 192], P(None, 'inner')
The draws below stay inside these ranges and needn't reach their ends.
Inputs may be any that keep to these rules, and one draw needn't show every extreme that they name: shocks of the inner short rate, one per path, year, date and scenario. Slot j holds cohort owner_map[j]; every cohort is held in exactly one slot.
All inputs are finite; a program needn't handle non-finite values.
Results may differ from the reference program's by a relative error of at most 0.0001.
Values sent between devices are 32-bit elements; how exact they have to be, the bound alone decides.
A program may use at most 64 MiB of HBM per device.

```python
import math
import jax
import jax.numpy as jnp
from jax import lax

DATES = 2
YEARS = 60
COHORTS = 192
RUNGS = 4
SCEN = 32
PATHS = 1024


def draw_shocks(key, part):
    bulk_key, jitter_key = jax.random.split(key, 2)
    bulk_shocks = jnp.clip(jax.random.normal(bulk_key, (SCEN, DATES, YEARS - 1, PATHS), jnp.float32), -5.0, 5.0)
    offset = 0.25 + 0.5 * jax.random.uniform(jitter_key, (SCEN, DATES, 1, PATHS), jnp.float32)
    strata = (jnp.arange(PATHS, dtype=jnp.float32)[None, None, None, :] + offset) / PATHS
    lead_shocks = jnp.clip(jnp.log(strata / (1.0 - strata)) / 1.702, -5.0, 5.0)
    return jnp.concatenate([lead_shocks, bulk_shocks], axis=2)


def draw_node_rate(key, part):
    grid_key, noise_key = jax.random.split(key, 2)
    grid_jitter = jax.random.uniform(grid_key, (SCEN, 1), jnp.float32)
    base_rate = -0.01 + 0.055 * (jnp.arange(SCEN, dtype=jnp.float32)[:, None] + grid_jitter) / SCEN
    rate_noise = 0.004 * jnp.clip(jax.random.normal(noise_key, (SCEN, DATES), jnp.float32), -3.0, 3.0)
    date_steps = jnp.arange(DATES, dtype=jnp.float32)[None, :]
    return base_rate + date_steps * rate_noise


def with_ends(drawn, own_key, smallest, largest):
    extent = drawn.shape
    spot = [jax.random.randint(jax.random.fold_in(own_key, axis), (), 0, extent[axis]) for axis in range(len(extent))]
    drawn = drawn.at[tuple(spot)].set(smallest)
    longest = extent.index(max(extent))
    spot[longest] = (spot[longest] + 1) % extent[longest]
    return drawn.at[tuple(spot)].set(largest)


def levels(stream_key, dims, cuts, low, largest):
    def one(dim, shards_of):
        steps = jax.random.uniform(jax.random.fold_in(jax.random.fold_in(stream_key, 6), dim), (shards_of,), jnp.float32, low / len(cuts), largest / len(cuts))
        return jnp.repeat(jnp.exp(steps), dims[dim] // shards_of).reshape((-1,) + (1,) * (len(dims) - dim - 1))

    factor_of = one(*cuts[0])
    for cut in cuts[1:]:
        factor_of = factor_of * one(*cut)
    return factor_of


def setup_inputs(seed: int = 0) -> dict:
    arg_keys = jax.random.split(jax.random.key(seed), 7)
    shocks = draw_shocks(jax.random.fold_in(arg_keys[6], 71), 0)
    node_rate = draw_node_rate(jax.random.fold_in(arg_keys[6], 71), 0)
    ladder_rung = with_ends(jax.random.randint(arg_keys[2], (SCEN, DATES), 0, RUNGS), jax.random.fold_in(arg_keys[2], 1), 0, RUNGS - 1).astype(jnp.int32)
    cash_flows = jnp.clip(jnp.exp(jax.random.uniform(arg_keys[3], (YEARS, COHORTS), jnp.float32, math.log(0.005), math.log(0.05))), 0.005, 0.05)
    owner_map = jax.random.permutation(arg_keys[4], COHORTS).astype(jnp.int32)
    capital = jnp.clip(0.3 + 1.2 * jax.random.uniform(arg_keys[5], (SCEN, COHORTS), jnp.float32) ** levels(arg_keys[5], (SCEN, COHORTS), ((0, 4), (1, 8)), -0.2, 0.2), 0.3, 1.5)
    return {"shocks": shocks, "node_rate": node_rate, "ladder_rung": ladder_rung, "cash_flows": cash_flows, "owner_map": owner_map, "capital": capital}


REVERT = 0.05
LONG_LEVEL = 0.025
VOLATILITY = 0.01
EPSILON = 1e-06

def year_tables(year_count):
    year_index = jnp.arange(year_count, dtype=jnp.float32)
    later_year = year_index[None, :]
    early_year = year_index[:, None]
    decay_rate = 1.0 - REVERT
    weights = jnp.where(early_year <= later_year, (1.0 - jnp.power(decay_rate, later_year + 1.0 - early_year)) / REVERT, 0.0)
    counts = year_index + 1.0
    drift_ramp = decay_rate * (1.0 - jnp.power(decay_rate, counts)) / REVERT
    return (counts, drift_ramp, weights)

def discount(node_rates, shocks_now):
    counts, drift_ramp, weights = year_tables(shocks_now.shape[1])
    drift_part = counts[None, :] * LONG_LEVEL + (node_rates[:, None] - LONG_LEVEL) * drift_ramp[None, :]
    shock_sums = jnp.einsum('jk,sjp->skp', weights, shocks_now, precision=lax.Precision.HIGHEST)
    return jnp.exp(-(drift_part[:, :, None] + VOLATILITY * shock_sums))

def ladder(funding_ratio, rung_level):
    floor_level = 0.9 + 0.1 * rung_level
    full_index = 0.01 + 0.005 * rung_level
    return full_index * jnp.clip((funding_ratio - floor_level) / 0.4, 0.0, 1.0)

def indexed_value(slot_flows, disc_one, index_one):
    year_count = jnp.arange(slot_flows.shape[0], dtype=jnp.float32) + 1.0
    growth = jnp.exp(year_count[:, None, None] * jnp.log1p(index_one)[None, :, :])
    return lax.optimization_barrier(jnp.sum(slot_flows[:, :, None] * disc_one[:, None, :] * growth, axis=0))

def reference(shocks, node_rate, ladder_rung, cash_flows, owner_map, capital):
    slot_flows = cash_flows[:, owner_map]
    holdings = capital
    values, spreads, fund_terms = ([], [], [])
    for date_index in range(DATES):
        discounts = discount(node_rate[:, date_index], shocks[:, date_index])
        nominal = jnp.einsum('kc,skp->scp', slot_flows, discounts, precision=lax.Precision.HIGHEST)
        rung_level = ladder_rung[:, date_index].astype(jnp.float32)
        fund_ratio = lax.optimization_barrier(jnp.sum(holdings, axis=1))[:, None] / lax.optimization_barrier(jnp.sum(nominal, axis=1))
        fund_terms.append(100.0 * lax.optimization_barrier(jnp.mean(ladder(fund_ratio, rung_level[:, None]), axis=1)))
        cohort_index = ladder(holdings[:, :, None] / nominal, rung_level[:, None, None])
        indexed = lax.map(lambda pieces: indexed_value(slot_flows, pieces[0], pieces[1]), (discounts, cohort_index))
        mean_value = lax.optimization_barrier(jnp.mean(indexed, axis=2))
        shortfall = jnp.minimum(indexed - mean_value[:, :, None], 0.0)
        spreads.append(jnp.sqrt(lax.optimization_barrier(jnp.mean(shortfall * shortfall, axis=2)) + EPSILON))
        values.append(mean_value)
        holdings = mean_value
    cohort_value = jnp.stack(values, axis=1)
    cohort_downside = jnp.stack(spreads, axis=1)
    fund_indexation = jnp.stack(fund_terms, axis=1)
    cohort_summary = lax.optimization_barrier(jnp.mean(cohort_value, axis=0))
    return (cohort_value, cohort_downside, fund_indexation, cohort_summary)
```

```python
from functools import partial

import jax
import jax.numpy as jnp
import ml_dtypes
import numpy as np
from jax import lax
from jax.experimental import pallas as pl
from jax.experimental.pallas import tpu as pltpu
from jax.sharding import PartitionSpec as P

MESH = pl.DeviceIdType.MESH
F32 = jnp.float32
BF16 = jnp.bfloat16

REVERT = 0.05
LONG_LEVEL = 0.025
VOLATILITY = 0.01
EPSILON = 1e-06
TOP_INDEX = 0.025


def split_bf16(table):
    high = table.astype(ml_dtypes.bfloat16)
    low = (table - high.astype(np.float64)).astype(ml_dtypes.bfloat16)
    return high, low


def discount_table(years, pad):
    decay = 1.0 - REVERT
    year = np.arange(years, dtype=np.float64)
    weights = np.where(
        year[:, None] <= year[None, :],
        (1.0 - decay ** np.maximum(year[None, :] + 1.0 - year[:, None], 0.0)) / REVERT,
        0.0,
    )
    count = year + 1.0
    ramp = decay * (1.0 - decay**count) / REVERT
    one = np.zeros((pad, pad))
    one[:years, :years] = -VOLATILITY * weights
    one[years, :years] = -LONG_LEVEL * (count - ramp)
    one[years + 1, :years] = -ramp
    high, low = split_bf16(one)
    rest = one - high.astype(np.float64) - low.astype(np.float64)
    one[years + 2] = rest[years]
    high, low = split_bf16(one)
    full = np.zeros((2, 4 * pad, 4 * pad), ml_dtypes.bfloat16)
    for which, part in enumerate((high, low)):
        for row in (0, 2 * pad):
            for copy in (0, pad):
                full[which, row : row + pad, copy : copy + pad] = part
                full[which, row + pad : row + 2 * pad, 2 * pad + copy : 3 * pad + copy] = part
    return full


def growth_table(years, pad):
    k = np.arange(years, dtype=np.float64) + 1.0
    probe = np.linspace(0.0, 1.0, 2001)
    exact = np.exp(k[:, None] * np.log1p(TOP_INDEX * probe)[None, :])
    for degree in range(3, 40):
        node = 0.5 + 0.5 * np.cos(np.pi * (np.arange(degree) + 0.5) / degree)
        quotient = np.expm1(k[:, None] * np.log1p(TOP_INDEX * node)[None, :]) / node
        cheb = np.polynomial.chebyshev.chebfit(2.0 * node - 1.0, quotient.T, degree - 1)
        table = np.zeros((degree + 1, years))
        table[0] = 1.0
        for i in range(years):
            line = np.polynomial.Chebyshev(cheb[:, i], domain=[0.0, 1.0]).convert(
                kind=np.polynomial.Polynomial, domain=[-1, 1], window=[-1, 1]
            )
            table[1 : 1 + len(line.coef), i] = line.coef
        found = np.zeros_like(exact)
        for m in range(degree, -1, -1):
            found = found * probe[None, :] + table[m][:, None]
        if np.max(np.abs(found / exact - 1.0)) < 2.0**-25:
            break
    out = np.zeros((degree + 1, pad, 128), np.float32)
    out[:, :years] = table[:, :, None]
    return out


def kernel(
    n_in, n_out, years, pad, cohorts, lanes, terms,
    rate_ref, rung_ref, shock_ref, flow_ref, owner_ref, capital_ref, weight_ref, growth_ref,
    value_ref, down_ref, fund_ref, summary_ref,
    lhs, gmat, coef, inverse, vals, hold, send, recv, sum_send, sum_recv,
    send_sem, recv_sem, osend_sem, orecv_sem,
):
    scen, dates, _, paths = shock_ref.shape
    own = capital_ref.shape[1]
    total = paths * n_in
    me = lax.axis_index("inner")
    me_out = lax.axis_index("outer")
    barrier = pltpu.get_barrier_semaphore()
    for o in range(1, n_in):
        pl.semaphore_signal(barrier, 1, device_id={"inner": lax.rem(me + o, n_in)}, device_id_type=MESH)
    for o in range(1, n_out):
        pl.semaphore_signal(barrier, 1, device_id={"outer": lax.rem(me_out + o, n_out)}, device_id_type=MESH)

    lane = lax.broadcasted_iota(jnp.int32, (scen, lanes), 1)
    is_slot = lane < cohorts

    def inner_copy(r, o):
        return pltpu.make_async_remote_copy(
            src_ref=send.at[r],
            dst_ref=recv.at[r, me],
            send_sem=send_sem.at[r, o - 1],
            recv_sem=recv_sem.at[r, o - 1],
            device_id={"inner": lax.rem(me + o, n_in)},
            device_id_type=MESH,
        )

    def start(r):
        for o in range(1, n_in):
            inner_copy(r, o).start()
        recv[r, me] = send[r]

    def finish(r):
        for o in range(1, n_in):
            inner_copy(r, o).wait_recv()
        out = recv[r, 0]
        for i in range(1, n_in):
            out = out + recv[r, i]
        return out

    def set_hold(held):
        fund = jnp.sum(jnp.where(is_slot, held, 0.0), axis=1, keepdims=True)
        hold[...] = jnp.where(is_slot, held, fund)

    def discounts(t):
        def body(i, carry):
            row4 = lax.broadcasted_iota(jnp.int32, (pad - years, paths), 0)
            parts = []
            for h in range(2):
                s = 2 * i + h
                rate = rate_ref[s, t]
                tail = jnp.where(row4 == 1, rate, jnp.where(row4 < 3, 1.0, 0.0)).astype(F32)
                parts += [shock_ref[s, t], tail]
            x = jnp.concatenate(parts, axis=0).T
            high = x.astype(BF16)
            low = (x - high.astype(F32)).astype(BF16)
            both = jnp.concatenate([high, low], axis=1)
            e = jnp.dot(both, weight_ref[0], preferred_element_type=F32)
            e = e + jnp.dot(both, weight_ref[1], preferred_element_type=F32)
            d = jnp.exp(e)
            dh = d.astype(BF16)
            dl = (d - dh.astype(F32)).astype(BF16)
            for h in range(2):
                rows = pl.ds(pl.multiple_of((2 * i + h) * paths, paths), paths)
                lhs[t, rows, 0 : 2 * pad] = dh[:, 2 * pad * h : 2 * pad * (h + 1)]
                lhs[t, rows, 2 * pad : 4 * pad] = dl[:, 2 * pad * h : 2 * pad * (h + 1)]
            return carry

        lax.fori_loop(0, scen // 2, body, 0)

    def coefficients(t):
        def body(m, carry):
            coef[m] = jnp.dot(lhs[t], gmat[m], preferred_element_type=F32)
            return carry

        lax.fori_loop(0, terms, body, 0)

        def body2(s, carry):
            rows = pl.ds(pl.multiple_of(s * paths, paths), paths)
            inverse[rows, :] = 1.0 / coef[0, rows, :]
            return carry

        lax.fori_loop(0, scen, body2, 0)

    def evaluate(t, r):
        for s in range(scen):
            rows = slice(s * paths, (s + 1) * paths)
            rung = rung_ref[s, t].astype(F32)
            top = (0.01 + 0.005 * rung) * (1.0 / TOP_INDEX)
            scale = top * 2.5
            shift = (0.9 + 0.1 * rung) * scale
            for c in range(0, lanes, 128):
                cols = slice(c, c + 128)
                y = (hold[slice(s, s + 1), cols] * scale) * inverse[rows, cols] - shift
                y = jnp.minimum(jnp.maximum(y, 0.0), top)
                v = coef[terms - 1, rows, cols]
                for m in range(terms - 2, -1, -1):
                    v = v * y + coef[m, rows, cols]
                vals[t, rows, cols] = v
                out = jnp.sum(v, axis=0, keepdims=True)
                if c + 128 > cohorts:
                    here = c + lax.broadcasted_iota(jnp.int32, (1, 128), 1) < cohorts
                    out = jnp.where(here, out, jnp.sum(y, axis=0, keepdims=True))
                send[r, slice(s, s + 1), cols] = out

    def shortfalls(t, r, mean_scr):
        for s in range(scen):
            rows = slice(s * paths, (s + 1) * paths)
            for c in range(0, lanes, 128):
                cols = slice(c, c + 128)
                short = jnp.minimum(vals[t, rows, cols] - mean_scr[slice(s, s + 1), cols], 0.0)
                send[r, slice(s, s + 1), cols] = jnp.sum(short * short, axis=0, keepdims=True)

    def mine(full):
        return pltpu.roll(full, lax.rem(lanes - own * me, lanes), 1)[:, :own]

    hold[...] = jnp.zeros_like(hold)
    hold[:, 0:own] = capital_ref[...]
    send[0] = pltpu.roll(hold[...], own * me, 1)

    cash = jnp.concatenate([flow_ref[...], jnp.zeros((pad - years, cohorts), F32)], axis=0)
    p0 = cash.astype(BF16)
    rest = cash - p0.astype(F32)
    p1 = rest.astype(BF16)
    p2 = (rest - p1.astype(F32)).astype(BF16)
    ids = lax.broadcasted_iota(jnp.int32, (cohorts, lanes), 0)
    slot = lax.broadcasted_iota(jnp.int32, (cohorts, lanes), 1)
    owner_row = jnp.concatenate([owner_ref[...], jnp.zeros((1, lanes - cohorts), jnp.int32)], axis=1)
    picker = jnp.where((ids == owner_row) | (slot >= cohorts), 1.0, 0.0).astype(BF16)
    flows = jnp.dot(p0, picker, preferred_element_type=F32)
    flows = flows + jnp.dot(p1, picker, preferred_element_type=F32)
    flows = flows + jnp.dot(p2, picker, preferred_element_type=F32)
    for m in range(terms):
        for c in range(0, lanes, 128):
            g = flows[:, c : c + 128] * growth_ref[m]
            gh = g.astype(BF16)
            gl = (g - gh.astype(F32)).astype(BF16)
            for q in range(2):
                gmat[m, 2 * pad * q : 2 * pad * q + pad, c : c + 128] = gh
                gmat[m, 2 * pad * q + pad : 2 * pad * (q + 1), c : c + 128] = gl

    pl.semaphore_wait(barrier, n_in - 1 + n_out - 1)
    start(0)
    for t in range(dates):
        discounts(t)
    coefficients(0)
    set_hold(finish(0))
    means = []
    funds = []
    for t in range(dates):
        r = 1 + t
        evaluate(t, r)
        start(r)
        if t + 1 < dates:
            coefficients(t + 1)
        if t > 0:
            shortfalls(t - 1, dates + t, hold)
            start(dates + t)
        sums = finish(r)
        mean = jnp.where(is_slot, sums / total, 0.0)
        means.append(mean)
        funds.append((sums[:, cohorts : cohorts + 1] / total) * (100.0 * TOP_INDEX))
        set_hold(mean)
    shortfalls(dates - 1, 2 * dates, hold)
    start(2 * dates)

    for t in range(dates):
        sum_send[t : t + 1, :] = jnp.sum(means[t], axis=0, keepdims=True)

    def outer_copy(o):
        return pltpu.make_async_remote_copy(
            src_ref=sum_send,
            dst_ref=sum_recv.at[me_out],
            send_sem=osend_sem.at[o - 1],
            recv_sem=orecv_sem.at[o - 1],
            device_id={"outer": lax.rem(me_out + o, n_out)},
            device_id_type=MESH,
        )

    for o in range(1, n_out):
        outer_copy(o).start()
    sum_recv[me_out] = sum_send[...]

    for t in range(dates):
        fund_ref[:, t : t + 1] = funds[t]
        part = mine(means[t])
        for s in range(scen):
            value_ref[s, t : t + 1, :] = part[s : s + 1]
    for o in range(1, n_out):
        outer_copy(o).wait_recv()
    summed = sum_recv[0]
    for i in range(1, n_out):
        summed = summed + sum_recv[i]
    summary_ref[...] = mine(summed / (scen * n_out))[0:dates]
    for t in range(dates):
        part = mine(jnp.sqrt(finish(dates + 1 + t) / total + EPSILON))
        for s in range(scen):
            down_ref[s, t : t + 1, :] = part[s : s + 1]
    for r in range(2 * dates + 1):
        for o in range(1, n_in):
            inner_copy(r, o).wait_send()
    for o in range(1, n_out):
        outer_copy(o).wait_send()


def shards(n_in, n_out, shocks, node_rate, ladder_rung, cash_flows, owner_map, capital):
    scen, dates, years, paths = shocks.shape
    cohorts = cash_flows.shape[1]
    own = capital.shape[1]
    pad = 64
    lanes = -(-(cohorts + 1) // 128) * 128
    weight = discount_table(years, pad)
    growth = growth_table(years, pad)
    terms = growth.shape[0]
    vmem = pl.BlockSpec(memory_space=pltpu.VMEM)
    smem = pl.BlockSpec(memory_space=pltpu.SMEM)
    rounds = 2 * dates + 1
    rows = scen * paths
    return pl.pallas_call(
        partial(kernel, n_in, n_out, years, pad, cohorts, lanes, terms),
        out_shape=(
            jax.ShapeDtypeStruct((scen, dates, own), F32),
            jax.ShapeDtypeStruct((scen, dates, own), F32),
            jax.ShapeDtypeStruct((scen, dates), F32),
            jax.ShapeDtypeStruct((dates, own), F32),
        ),
        in_specs=[smem, smem] + [vmem] * 6,
        out_specs=(vmem,) * 4,
        scratch_shapes=[
            pltpu.VMEM((dates, rows, 4 * pad), BF16),
            pltpu.VMEM((terms, 4 * pad, lanes), BF16),
            pltpu.VMEM((terms, rows, lanes), F32),
            pltpu.VMEM((rows, lanes), F32),
            pltpu.VMEM((dates, rows, lanes), F32),
            pltpu.VMEM((scen, lanes), F32),
            pltpu.VMEM((rounds, scen, lanes), F32),
            pltpu.VMEM((rounds, n_in, scen, lanes), F32),
            pltpu.VMEM((8, lanes), F32),
            pltpu.VMEM((n_out, 8, lanes), F32),
            pltpu.SemaphoreType.DMA((rounds, n_in)),
            pltpu.SemaphoreType.DMA((rounds, n_in)),
            pltpu.SemaphoreType.DMA((n_out,)),
            pltpu.SemaphoreType.DMA((n_out,)),
        ],
        compiler_params=pltpu.CompilerParams(
            collective_id=0, has_side_effects=True, vmem_limit_bytes=48 * 1024 * 1024
        ),
    )(node_rate, ladder_rung, shocks, cash_flows, owner_map.reshape(1, cohorts), capital, weight, growth)


def solution(mesh):
    return jax.shard_map(
        partial(shards, mesh.shape["inner"], mesh.shape["outer"]),
        mesh=mesh,
        in_specs=(
            P("outer", None, None, "inner"),
            P("outer", None),
            P("outer", None),
            P(),
            P(),
            P("outer", "inner"),
        ),
        out_specs=(
            P("outer", None, "inner"),
            P("outer", None, "inner"),
            P("outer", None),
            P(None, "inner"),
        ),
        check_vma=False,
    )
```

```python
from functools import partial

import jax
import jax.numpy as jnp
import ml_dtypes
import numpy as np
from jax import lax
from jax.experimental import pallas as pl
from jax.experimental.pallas import tpu as pltpu
from jax.sharding import PartitionSpec as P

MESH = pl.DeviceIdType.MESH
F32 = jnp.float32
BF16 = jnp.bfloat16

REVERT = 0.05
LONG_LEVEL = 0.025
VOLATILITY = 0.01
EPSILON = 1e-06
TOP_INDEX = 0.025


def split_bf16(table):
    high = table.astype(ml_dtypes.bfloat16)
    low = (table - high.astype(np.float64)).astype(ml_dtypes.bfloat16)
    return high, low


def discount_table(years, dates, pad):
    decay = 1.0 - REVERT
    year = np.arange(years, dtype=np.float64)
    weights = np.where(
        year[:, None] <= year[None, :],
        (1.0 - decay ** np.maximum(year[None, :] + 1.0 - year[:, None], 0.0)) / REVERT,
        0.0,
    )
    count = year + 1.0
    ramp = decay * (1.0 - decay**count) / REVERT
    used = years * dates
    one = np.zeros((2 * pad, 2 * pad * dates))
    for t in range(dates):
        for copy in (0, pad):
            cols = slice(2 * pad * t + copy, 2 * pad * t + copy + years)
            one[t:used:dates, cols] = -VOLATILITY * weights
            one[used, cols] = -LONG_LEVEL * (count - ramp)
            one[used + 2 + t, cols] = -ramp
    high, low = split_bf16(one)
    rest = one - high.astype(np.float64) - low.astype(np.float64)
    one[used + 1] = rest[used]
    high, low = split_bf16(one)
    return np.stack([high, low])


def growth_table(years, pad):
    k = np.arange(years, dtype=np.float64) + 1.0
    probe = np.linspace(0.0, 1.0, 2001)
    exact = np.exp(k[:, None] * np.log1p(TOP_INDEX * probe)[None, :])
    for degree in range(3, 40):
        node = 0.5 + 0.5 * np.cos(np.pi * (np.arange(degree) + 0.5) / degree)
        quotient = np.expm1(k[:, None] * np.log1p(TOP_INDEX * node)[None, :]) / node
        cheb = np.polynomial.chebyshev.chebfit(2.0 * node - 1.0, quotient.T, degree - 1)
        table = np.zeros((degree + 1, years))
        table[0] = 1.0
        for i in range(years):
            line = np.polynomial.Chebyshev(cheb[:, i], domain=[0.0, 1.0]).convert(
                kind=np.polynomial.Polynomial, domain=[-1, 1], window=[-1, 1]
            )
            table[1 : 1 + len(line.coef), i] = line.coef
        found = np.zeros_like(exact)
        for m in range(degree, -1, -1):
            found = found * probe[None, :] + table[m][:, None]
        if np.max(np.abs(found / exact - 1.0)) < 2.0**-25:
            break
    out = np.zeros((pad, 128), np.float32)
    out[:years, : degree + 1] = table.T
    return out, degree + 1


def kernel(
    n_in, n_out, years, pad, cohorts, lanes, terms,
    rate_hbm, rung_hbm, shock_hbm, flow_hbm, owner_hbm, capital_hbm, weight_hbm, growth_hbm,
    value_ref, down_ref, fund_ref, summary_ref,
    rate_ref, rung_ref, shock_ref, flow_ref, owner_ref, capital_ref, weight_ref, growth_ref,
    lhs, gmat, coef, inverse, vals, hold, send, recv, short, short_send, short_recv, sum_send, sum_recv,
    load_sem, send_sem, recv_sem, ssend_sem, srecv_sem, osend_sem, orecv_sem,
):
    dates, scen = rate_hbm.shape
    paths = shock_hbm.shape[1]
    used = dates * years
    own = capital_hbm.shape[1]
    total = paths * n_in
    me = lax.axis_index("inner")
    me_out = lax.axis_index("outer")
    loads = [
        pltpu.make_async_copy(source, target, load_sem.at[i])
        for i, (source, target) in enumerate((
            (capital_hbm, capital_ref), (flow_hbm, flow_ref), (owner_hbm, owner_ref), (growth_hbm, growth_ref),
            (rate_hbm, rate_ref), (weight_hbm, weight_ref), (shock_hbm, shock_ref), (rung_hbm, rung_ref),
        ))
    ]
    barrier = pltpu.get_barrier_semaphore()
    for o in range(1, n_in):
        pl.semaphore_signal(barrier, 1, device_id={"inner": lax.rem(me + o, n_in)}, device_id_type=MESH)
    for o in range(1, n_out):
        pl.semaphore_signal(barrier, 1, device_id={"outer": lax.rem(me_out + o, n_out)}, device_id_type=MESH)

    for load in loads:
        load.start()
    lane = lax.broadcasted_iota(jnp.int32, (scen, lanes), 1)
    is_slot = lane < cohorts

    def inner_copy(r, o):
        return pltpu.make_async_remote_copy(
            src_ref=send.at[r],
            dst_ref=recv.at[r, me],
            send_sem=send_sem.at[r, o - 1],
            recv_sem=recv_sem.at[r, o - 1],
            device_id={"inner": lax.rem(me + o, n_in)},
            device_id_type=MESH,
        )

    def start(r):
        for o in range(1, n_in):
            inner_copy(r, o).start()
        recv[r, me] = send[r]

    def finish(r):
        for o in range(1, n_in):
            inner_copy(r, o).wait_recv()
        out = recv[r, 0]
        for i in range(1, n_in):
            out = out + recv[r, i]
        return out

    def set_hold(held):
        fund = jnp.sum(jnp.where(is_slot, held, 0.0), axis=1, keepdims=True)
        hold[...] = jnp.where(is_slot, held, fund)

    def discounts():
        weights = [jnp.concatenate([weight_ref[i], weight_ref[i]], axis=0) for i in range(2)]
        row8 = lax.broadcasted_iota(jnp.int32, (2 * pad - used, paths), 0)
        for s in range(scen):
            tail = jnp.where(row8 < 2, 1.0, 0.0).astype(F32)
            for t in range(dates):
                tail = jnp.where(row8 == 2 + t, rate_ref[t, s], tail)
            x = jnp.concatenate([shock_ref[s * used : (s + 1) * used, :], tail], axis=0).T
            high = x.astype(BF16)
            low = (x - high.astype(F32)).astype(BF16)
            both = jnp.concatenate([high, low], axis=1)
            e = jnp.dot(both, weights[0], preferred_element_type=F32)
            e = e + jnp.dot(both, weights[1], preferred_element_type=F32)
            d = jnp.exp(e)
            dh = d.astype(BF16)
            dl = (d - dh.astype(F32)).astype(BF16)
            rows = slice(s * paths, (s + 1) * paths)
            for t in range(dates):
                lhs[t, rows, 0 : 2 * pad] = dh[:, 2 * pad * t : 2 * pad * (t + 1)]
                lhs[t, rows, 2 * pad : 4 * pad] = dl[:, 2 * pad * t : 2 * pad * (t + 1)]

    def coefficients(t):
        for m in range(terms):
            coef[m] = jnp.dot(lhs[t], gmat[m], preferred_element_type=F32)
            if m == 0:
                for s in range(scen):
                    rows = slice(s * paths, (s + 1) * paths)
                    nominal = coef[0, rows, :]
                    guess = pl.reciprocal(nominal, approx=True)
                    guess = guess * (2.0 - nominal * guess)
                    inverse[rows, :] = guess * (2.0 - nominal * guess)

    def evaluate(t, r):
        for s in range(scen):
            rows = slice(s * paths, (s + 1) * paths)
            rung = rung_ref[t, s].astype(F32)
            top = (0.01 + 0.005 * rung) * (1.0 / TOP_INDEX)
            scale = top * 2.5
            shift = (0.9 + 0.1 * rung) * scale
            for c in range(0, lanes, 128):
                cols = slice(c, c + 128)
                y = (hold[slice(s, s + 1), cols] * scale) * inverse[rows, cols] - shift
                y = jnp.minimum(jnp.maximum(y, 0.0), top)
                v = coef[terms - 1, rows, cols]
                for m in range(terms - 2, -1, -1):
                    v = v * y + coef[m, rows, cols]
                vals[t, rows, cols] = v
                out = jnp.sum(v, axis=0, keepdims=True)
                if c + 128 > cohorts:
                    here = c + lax.broadcasted_iota(jnp.int32, (1, 128), 1) < cohorts
                    out = jnp.where(here, out, jnp.sum(y, axis=0, keepdims=True))
                send[r, slice(s, s + 1), cols] = out

    def short_copy(t, o):
        return pltpu.make_async_remote_copy(
            src_ref=short_send.at[t, o - 1],
            dst_ref=short_recv.at[t, me],
            send_sem=ssend_sem.at[t, o - 1],
            recv_sem=srecv_sem.at[t, o - 1],
            device_id={"inner": lax.rem(me + o, n_in)},
            device_id_type=MESH,
        )

    def shortfalls(t):
        for s in range(scen):
            rows = slice(s * paths, (s + 1) * paths)
            for c in range(0, lanes, 128):
                cols = slice(c, c + 128)
                below = jnp.minimum(vals[t, rows, cols] - hold[s : s + 1, cols], 0.0)
                short[s : s + 1, cols] = jnp.sum(below * below, axis=0, keepdims=True)
        for o in range(1, n_in):
            short_send[t, o - 1] = of_device(short[...], lax.rem(me + o, n_in))
            short_copy(t, o).start()
        short_recv[t, me] = of_device(short[...], me)

    def of_device(full, device):
        return pltpu.roll(full, lax.rem(lanes - own * device, lanes), 1)[:, :128]

    def mine(full):
        return of_device(full, me)[:, :own]

    for load in loads[:4]:
        load.wait()
    hold[...] = jnp.zeros_like(hold)
    hold[:, 0:own] = capital_ref[...]
    send[0] = pltpu.roll(hold[...], own * me, 1)

    cash = jnp.concatenate([flow_ref[...], jnp.zeros((pad - years, cohorts), F32)], axis=0)
    p0 = cash.astype(BF16)
    rest = cash - p0.astype(F32)
    p1 = rest.astype(BF16)
    p2 = (rest - p1.astype(F32)).astype(BF16)
    ids = lax.broadcasted_iota(jnp.int32, (cohorts, lanes), 0)
    slot = lax.broadcasted_iota(jnp.int32, (cohorts, lanes), 1)
    owner_row = jnp.concatenate([owner_ref[...], jnp.zeros((1, lanes - cohorts), jnp.int32)], axis=1)
    picker = jnp.where((ids == owner_row) | (slot >= cohorts), 1.0, 0.0).astype(BF16)
    flows = jnp.dot(p0, picker, preferred_element_type=F32)
    flows = flows + jnp.dot(p1, picker, preferred_element_type=F32)
    flows = flows + jnp.dot(p2, picker, preferred_element_type=F32)
    for m in range(terms):
        for c in range(0, lanes, 128):
            g = flows[:, c : c + 128] * growth_ref[:, m : m + 1]
            gh = g.astype(BF16)
            gl = (g - gh.astype(F32)).astype(BF16)
            for q in range(2):
                gmat[m, 2 * pad * q : 2 * pad * q + pad, c : c + 128] = gh
                gmat[m, 2 * pad * q + pad : 2 * pad * (q + 1), c : c + 128] = gl

    pl.semaphore_wait(barrier, n_in - 1 + n_out - 1)
    start(0)
    for load in loads[4:]:
        load.wait()
    discounts()
    coefficients(0)
    set_hold(finish(0))
    means = []
    funds = []
    for t in range(dates):
        r = 1 + t
        evaluate(t, r)
        start(r)
        if t + 1 < dates:
            coefficients(t + 1)
        if t > 0:
            shortfalls(t - 1)
        sums = finish(r)
        mean = jnp.where(is_slot, sums / total, 0.0)
        means.append(mean)
        funds.append((sums[:, cohorts : cohorts + 1] / total).T * (100.0 * TOP_INDEX))
        set_hold(mean)
    shortfalls(dates - 1)

    for t in range(dates):
        sum_send[t : t + 1, :] = jnp.sum(means[t], axis=0, keepdims=True)

    def outer_copy(o):
        return pltpu.make_async_remote_copy(
            src_ref=sum_send,
            dst_ref=sum_recv.at[me_out],
            send_sem=osend_sem.at[o - 1],
            recv_sem=orecv_sem.at[o - 1],
            device_id={"outer": lax.rem(me_out + o, n_out)},
            device_id_type=MESH,
        )

    for o in range(1, n_out):
        outer_copy(o).start()
    sum_recv[me_out] = sum_send[...]

    for t in range(dates):
        fund_ref[t : t + 1, :] = funds[t]
        part = mine(means[t])
        for s in range(scen):
            value_ref[s, t : t + 1, :] = part[s : s + 1]
    for o in range(1, n_out):
        outer_copy(o).wait_recv()
    summed = sum_recv[0]
    for i in range(1, n_out):
        summed = summed + sum_recv[i]
    summary_ref[...] = mine(summed / (scen * n_out))[0:dates]
    for t in range(dates):
        for o in range(1, n_in):
            short_copy(t, o).wait_recv()
        squares = short_recv[t, 0]
        for i in range(1, n_in):
            squares = squares + short_recv[t, i]
        part = jnp.sqrt(squares[:, :own] / total + EPSILON)
        for s in range(scen):
            down_ref[s, t : t + 1, :] = part[s : s + 1]
    for o in range(1, n_in):
        for r in range(dates + 1):
            inner_copy(r, o).wait_send()
        for t in range(dates):
            short_copy(t, o).wait_send()
    for o in range(1, n_out):
        outer_copy(o).wait_send()


def shards(n_in, n_out, shocks, node_rate, ladder_rung, cash_flows, owner_map, capital):
    scen, dates, years, paths = shocks.shape
    cohorts = cash_flows.shape[1]
    own = capital.shape[1]
    pad = 64
    lanes = -(-(cohorts + 1) // 128) * 128
    weight = discount_table(years, dates, pad)
    growth, terms = growth_table(years, pad)
    by_year = jnp.transpose(shocks, (0, 2, 1, 3)).reshape(scen * years * dates, paths)
    vmem = pl.BlockSpec(memory_space=pltpu.VMEM)
    hbm = pl.BlockSpec(memory_space=pltpu.HBM)
    rounds = dates + 1
    rows = scen * paths
    results = pl.pallas_call(
        partial(kernel, n_in, n_out, years, pad, cohorts, lanes, terms),
        out_shape=(
            jax.ShapeDtypeStruct((scen, dates, own), F32),
            jax.ShapeDtypeStruct((scen, dates, own), F32),
            jax.ShapeDtypeStruct((dates, scen), F32),
            jax.ShapeDtypeStruct((dates, own), F32),
        ),
        in_specs=[hbm] * 8,
        out_specs=(vmem,) * 4,
        scratch_shapes=[
            pltpu.SMEM((dates, scen), F32),
            pltpu.SMEM((dates, scen), jnp.int32),
            pltpu.VMEM(by_year.shape, F32),
            pltpu.VMEM((years, cohorts), F32),
            pltpu.VMEM((1, cohorts), jnp.int32),
            pltpu.VMEM((scen, own), F32),
            pltpu.VMEM(weight.shape, BF16),
            pltpu.VMEM(growth.shape, F32),
            pltpu.VMEM((dates, rows, 4 * pad), BF16),
            pltpu.VMEM((terms, 4 * pad, lanes), BF16),
            pltpu.VMEM((terms, rows, lanes), F32),
            pltpu.VMEM((rows, lanes), F32),
            pltpu.VMEM((dates, rows, lanes), F32),
            pltpu.VMEM((scen, lanes), F32),
            pltpu.VMEM((rounds, scen, lanes), F32),
            pltpu.VMEM((rounds, n_in, scen, lanes), F32),
            pltpu.VMEM((scen, lanes), F32),
            pltpu.VMEM((dates, n_in, scen, 128), F32),
            pltpu.VMEM((dates, n_in, scen, 128), F32),
            pltpu.VMEM((8, lanes), F32),
            pltpu.VMEM((n_out, 8, lanes), F32),
            pltpu.SemaphoreType.DMA((8,)),
            pltpu.SemaphoreType.DMA((rounds, n_in)),
            pltpu.SemaphoreType.DMA((rounds, n_in)),
            pltpu.SemaphoreType.DMA((dates, n_in)),
            pltpu.SemaphoreType.DMA((dates, n_in)),
            pltpu.SemaphoreType.DMA((n_out,)),
            pltpu.SemaphoreType.DMA((n_out,)),
        ],
        compiler_params=pltpu.CompilerParams(
            collective_id=0, has_side_effects=True, vmem_limit_bytes=55168 * 1024
        ),
    )(node_rate.T, ladder_rung.T, by_year, cash_flows, owner_map.reshape(1, cohorts), capital, weight, growth)
    value, down, fund, summary = pl.pallas_call(
        deliver,
        out_shape=tuple(jax.ShapeDtypeStruct(x.shape, x.dtype) for x in results),
        in_specs=[pl.BlockSpec(memory_space=pl.ANY)] * 4,
        out_specs=(pl.BlockSpec(memory_space=pl.ANY),) * 4,
        scratch_shapes=[pltpu.SemaphoreType.DMA((4,))],
        compiler_params=pltpu.CompilerParams(vmem_limit_bytes=1024 * 1024),
    )(*results)
    return value, down, fund.T, summary


def deliver(*refs):
    count = (len(refs) - 1) // 2
    copies = [pltpu.make_async_copy(refs[i], refs[count + i], refs[-1].at[i]) for i in range(count)]
    for copy in copies:
        copy.start()
    for copy in copies:
        copy.wait()


def solution(mesh):
    return jax.shard_map(
        partial(shards, mesh.shape["inner"], mesh.shape["outer"]),
        mesh=mesh,
        in_specs=(
            P("outer", None, None, "inner"),
            P("outer", None),
            P("outer", None),
            P(),
            P(),
            P("outer", "inner"),
        ),
        out_specs=(
            P("outer", None, "inner"),
            P("outer", None, "inner"),
            P("outer", None),
            P(None, "inner"),
        ),
        check_vma=False,
    )
```

```python
from functools import partial

import jax
import jax.numpy as jnp
import ml_dtypes
import numpy as np
from jax import lax
from jax.experimental import pallas as pl
from jax.experimental.pallas import tpu as pltpu
from jax.sharding import PartitionSpec as P

MESH = pl.DeviceIdType.MESH
F32 = jnp.float32
BF16 = jnp.bfloat16

REVERT = 0.05
LONG_LEVEL = 0.025
VOLATILITY = 0.01
EPSILON = 1e-06
TOP_INDEX = 0.025


def split_bf16(table):
    high = table.astype(ml_dtypes.bfloat16)
    low = (table - high.astype(np.float64)).astype(ml_dtypes.bfloat16)
    return high, low


def discount_table(years, dates, pad):
    decay = 1.0 - REVERT
    year = np.arange(years, dtype=np.float64)
    weights = np.where(
        year[:, None] <= year[None, :],
        (1.0 - decay ** np.maximum(year[None, :] + 1.0 - year[:, None], 0.0)) / REVERT,
        0.0,
    )
    count = year + 1.0
    ramp = decay * (1.0 - decay**count) / REVERT
    used = years * dates
    one = np.zeros((2 * pad, 2 * pad * dates))
    for t in range(dates):
        for copy in (0, pad):
            cols = slice(2 * pad * t + copy, 2 * pad * t + copy + years)
            one[t:used:dates, cols] = -VOLATILITY * weights
            one[used, cols] = -LONG_LEVEL * (count - ramp)
            one[used + 2 + t, cols] = -ramp
    high, low = split_bf16(one)
    rest = one - high.astype(np.float64) - low.astype(np.float64)
    one[used + 1] = rest[used]
    high, low = split_bf16(one)
    return np.stack([high, low])


def growth_table(years, pad):
    k = np.arange(years, dtype=np.float64) + 1.0
    probe = np.linspace(0.0, 1.0, 2001)
    exact = np.exp(k[:, None] * np.log1p(TOP_INDEX * probe)[None, :])
    for degree in range(3, 40):
        node = 0.5 + 0.5 * np.cos(np.pi * (np.arange(degree) + 0.5) / degree)
        quotient = np.expm1(k[:, None] * np.log1p(TOP_INDEX * node)[None, :]) / node
        cheb = np.polynomial.chebyshev.chebfit(2.0 * node - 1.0, quotient.T, degree - 1)
        table = np.zeros((degree + 1, years))
        table[0] = 1.0
        for i in range(years):
            line = np.polynomial.Chebyshev(cheb[:, i], domain=[0.0, 1.0]).convert(
                kind=np.polynomial.Polynomial, domain=[-1, 1], window=[-1, 1]
            )
            table[1 : 1 + len(line.coef), i] = line.coef
        found = np.zeros_like(exact)
        for m in range(degree, -1, -1):
            found = found * probe[None, :] + table[m][:, None]
        if np.max(np.abs(found / exact - 1.0)) < 2.0**-25:
            break
    out = np.zeros((pad, 128), np.float32)
    out[:years, : degree + 1] = table.T
    return out, degree + 1


def kernel(
    n_in, n_out, years, pad, cohorts, lanes, terms,
    rate_hbm, rung_hbm, shock_hbm, flow_hbm, owner_hbm, capital_hbm, weight_hbm, growth_hbm,
    value_ref, down_ref, fund_ref, summary_ref,
    rate_ref, rung_ref, shock_ref, flow_ref, owner_ref, capital_ref, weight_ref, growth_ref,
    lhs, gmat, coef, inverse, vals, hold, send, recv, short, short_send, short_recv, sum_send, sum_recv,
    load_sem, send_sem, recv_sem, ssend_sem, srecv_sem, osend_sem, orecv_sem,
):
    dates, scen = rate_hbm.shape
    paths = shock_hbm.shape[1]
    used = dates * years
    own = capital_hbm.shape[1]
    total = paths * n_in
    me = lax.axis_index("inner")
    me_out = lax.axis_index("outer")
    loads = [
        pltpu.make_async_copy(source, target, load_sem.at[i])
        for i, (source, target) in enumerate((
            (capital_hbm, capital_ref), (flow_hbm, flow_ref), (owner_hbm, owner_ref), (growth_hbm, growth_ref),
            (rate_hbm, rate_ref), (weight_hbm, weight_ref), (shock_hbm, shock_ref), (rung_hbm, rung_ref),
        ))
    ]
    loads[0].start()
    barrier = pltpu.get_barrier_semaphore()
    for o in range(1, n_in):
        pl.semaphore_signal(barrier, 1, device_id={"inner": lax.rem(me + o, n_in)}, device_id_type=MESH)
    for o in range(1, n_out):
        pl.semaphore_signal(barrier, 1, device_id={"outer": lax.rem(me_out + o, n_out)}, device_id_type=MESH)

    for load in loads[1:]:
        load.start()
    lane = lax.broadcasted_iota(jnp.int32, (scen, lanes), 1)
    is_slot = lane < cohorts

    def inner_copy(r, o):
        return pltpu.make_async_remote_copy(
            src_ref=send.at[r],
            dst_ref=recv.at[r, me],
            send_sem=send_sem.at[r, o - 1],
            recv_sem=recv_sem.at[r, o - 1],
            device_id={"inner": lax.rem(me + o, n_in)},
            device_id_type=MESH,
        )

    def start(r):
        for o in range(1, n_in):
            inner_copy(r, o).start()
        recv[r, me] = send[r]

    def finish(r):
        for o in range(1, n_in):
            inner_copy(r, o).wait_recv()
        out = recv[r, 0]
        for i in range(1, n_in):
            out = out + recv[r, i]
        return out

    def set_hold(held):
        fund = jnp.sum(jnp.where(is_slot, held, 0.0), axis=1, keepdims=True)
        hold[...] = jnp.where(is_slot, held, fund)

    def discounts():
        weights = [jnp.concatenate([weight_ref[i], weight_ref[i]], axis=0) for i in range(2)]
        row8 = lax.broadcasted_iota(jnp.int32, (2 * pad - used, paths), 0)
        for s in range(scen):
            tail = jnp.where(row8 < 2, 1.0, 0.0).astype(F32)
            for t in range(dates):
                tail = jnp.where(row8 == 2 + t, rate_ref[t, s], tail)
            x = jnp.concatenate([shock_ref[s * used : (s + 1) * used, :], tail], axis=0).T
            high = x.astype(BF16)
            low = (x - high.astype(F32)).astype(BF16)
            both = jnp.concatenate([high, low], axis=1)
            e = jnp.dot(both, weights[0], preferred_element_type=F32)
            e = e + jnp.dot(both, weights[1], preferred_element_type=F32)
            d = jnp.exp(e)
            dh = d.astype(BF16)
            dl = (d - dh.astype(F32)).astype(BF16)
            rows = slice(s * paths, (s + 1) * paths)
            for t in range(dates):
                lhs[t, rows, 0 : 2 * pad] = dh[:, 2 * pad * t : 2 * pad * (t + 1)]
                lhs[t, rows, 2 * pad : 4 * pad] = dl[:, 2 * pad * t : 2 * pad * (t + 1)]

    def coefficients(t):
        for m in range(terms):
            coef[m] = jnp.dot(lhs[t], gmat[m], preferred_element_type=F32)
            if m == 0:
                for s in range(scen):
                    rows = slice(s * paths, (s + 1) * paths)
                    nominal = coef[0, rows, :]
                    guess = pl.reciprocal(nominal, approx=True)
                    guess = guess * (2.0 - nominal * guess)
                    inverse[rows, :] = guess * (2.0 - nominal * guess)

    def evaluate(t, r):
        for s in range(scen):
            rows = slice(s * paths, (s + 1) * paths)
            rung = rung_ref[t, s].astype(F32)
            top = (0.01 + 0.005 * rung) * (1.0 / TOP_INDEX)
            scale = top * 2.5
            shift = (0.9 + 0.1 * rung) * scale
            for c in range(0, lanes, 128):
                cols = slice(c, c + 128)
                y = (hold[slice(s, s + 1), cols] * scale) * inverse[rows, cols] - shift
                y = jnp.minimum(jnp.maximum(y, 0.0), top)
                v = coef[terms - 1, rows, cols]
                for m in range(terms - 2, -1, -1):
                    v = v * y + coef[m, rows, cols]
                vals[t, rows, cols] = v
                out = jnp.sum(v, axis=0, keepdims=True)
                if c + 128 > cohorts:
                    here = c + lax.broadcasted_iota(jnp.int32, (1, 128), 1) < cohorts
                    out = jnp.where(here, out, jnp.sum(y, axis=0, keepdims=True))
                send[r, slice(s, s + 1), cols] = out

    def short_copy(t, o):
        return pltpu.make_async_remote_copy(
            src_ref=short_send.at[t, o - 1],
            dst_ref=short_recv.at[t, me],
            send_sem=ssend_sem.at[t, o - 1],
            recv_sem=srecv_sem.at[t, o - 1],
            device_id={"inner": lax.rem(me + o, n_in)},
            device_id_type=MESH,
        )

    def shortfalls(t):
        for s in range(scen):
            rows = slice(s * paths, (s + 1) * paths)
            for c in range(0, lanes, 128):
                cols = slice(c, c + 128)
                below = jnp.minimum(vals[t, rows, cols] - hold[s : s + 1, cols], 0.0)
                short[s : s + 1, cols] = jnp.sum(below * below, axis=0, keepdims=True)
        for o in range(1, n_in):
            short_send[t, o - 1] = of_device(short[...], lax.rem(me + o, n_in))
            short_copy(t, o).start()
        short_recv[t, me] = of_device(short[...], me)

    def of_device(full, device):
        return pltpu.roll(full, lax.rem(lanes - own * device, lanes), 1)[:, :128]

    def mine(full):
        return of_device(full, me)[:, :own]

    loads[0].wait()
    hold[...] = jnp.zeros_like(hold)
    hold[:, 0:own] = capital_ref[...]
    send[0] = pltpu.roll(hold[...], own * me, 1)

    pl.semaphore_wait(barrier, n_in - 1 + n_out - 1)
    start(0)

    for load in loads[1:4]:
        load.wait()
    cash = jnp.concatenate([flow_ref[...], jnp.zeros((pad - years, cohorts), F32)], axis=0)
    p0 = cash.astype(BF16)
    rest = cash - p0.astype(F32)
    p1 = rest.astype(BF16)
    p2 = (rest - p1.astype(F32)).astype(BF16)
    ids = lax.broadcasted_iota(jnp.int32, (cohorts, lanes), 0)
    slot = lax.broadcasted_iota(jnp.int32, (cohorts, lanes), 1)
    owner_row = jnp.concatenate([owner_ref[...], jnp.zeros((1, lanes - cohorts), jnp.int32)], axis=1)
    picker = jnp.where((ids == owner_row) | (slot >= cohorts), 1.0, 0.0).astype(BF16)
    flows = jnp.dot(p0, picker, preferred_element_type=F32)
    flows = flows + jnp.dot(p1, picker, preferred_element_type=F32)
    flows = flows + jnp.dot(p2, picker, preferred_element_type=F32)
    for m in range(terms):
        for c in range(0, lanes, 128):
            g = flows[:, c : c + 128] * growth_ref[:, m : m + 1]
            gh = g.astype(BF16)
            gl = (g - gh.astype(F32)).astype(BF16)
            for q in range(2):
                gmat[m, 2 * pad * q : 2 * pad * q + pad, c : c + 128] = gh
                gmat[m, 2 * pad * q + pad : 2 * pad * (q + 1), c : c + 128] = gl

    for load in loads[4:]:
        load.wait()
    discounts()
    coefficients(0)
    set_hold(finish(0))
    means = []
    funds = []
    for t in range(dates):
        r = 1 + t
        evaluate(t, r)
        start(r)
        if t + 1 < dates:
            coefficients(t + 1)
        if t > 0:
            shortfalls(t - 1)
        sums = finish(r)
        mean = jnp.where(is_slot, sums / total, 0.0)
        means.append(mean)
        funds.append((sums[:, cohorts : cohorts + 1] / total).T * (100.0 * TOP_INDEX))
        set_hold(mean)
    shortfalls(dates - 1)

    for t in range(dates):
        sum_send[t : t + 1, :] = jnp.sum(means[t], axis=0, keepdims=True)

    def outer_copy(o):
        return pltpu.make_async_remote_copy(
            src_ref=sum_send,
            dst_ref=sum_recv.at[me_out],
            send_sem=osend_sem.at[o - 1],
            recv_sem=orecv_sem.at[o - 1],
            device_id={"outer": lax.rem(me_out + o, n_out)},
            device_id_type=MESH,
        )

    for o in range(1, n_out):
        outer_copy(o).start()
    sum_recv[me_out] = sum_send[...]

    for t in range(dates):
        fund_ref[t : t + 1, :] = funds[t]
        part = mine(means[t])
        for s in range(scen):
            value_ref[s, t : t + 1, :] = part[s : s + 1]
    for o in range(1, n_out):
        outer_copy(o).wait_recv()
    summed = sum_recv[0]
    for i in range(1, n_out):
        summed = summed + sum_recv[i]
    summary_ref[...] = mine(summed / (scen * n_out))[0:dates]
    for t in range(dates):
        for o in range(1, n_in):
            short_copy(t, o).wait_recv()
        squares = short_recv[t, 0]
        for i in range(1, n_in):
            squares = squares + short_recv[t, i]
        part = jnp.sqrt(squares[:, :own] / total + EPSILON)
        for s in range(scen):
            down_ref[s, t : t + 1, :] = part[s : s + 1]
    for o in range(1, n_in):
        for r in range(dates + 1):
            inner_copy(r, o).wait_send()
        for t in range(dates):
            short_copy(t, o).wait_send()
    for o in range(1, n_out):
        outer_copy(o).wait_send()


def shards(n_in, n_out, shocks, node_rate, ladder_rung, cash_flows, owner_map, capital):
    scen, dates, years, paths = shocks.shape
    cohorts = cash_flows.shape[1]
    own = capital.shape[1]
    pad = 64
    lanes = -(-(cohorts + 1) // 128) * 128
    weight = discount_table(years, dates, pad)
    growth, terms = growth_table(years, pad)
    by_year = jnp.transpose(shocks, (0, 2, 1, 3)).reshape(scen * years * dates, paths)
    vmem = pl.BlockSpec(memory_space=pltpu.VMEM)
    hbm = pl.BlockSpec(memory_space=pltpu.HBM)
    rounds = dates + 1
    rows = scen * paths
    results = pl.pallas_call(
        partial(kernel, n_in, n_out, years, pad, cohorts, lanes, terms),
        out_shape=(
            jax.ShapeDtypeStruct((scen, dates, own), F32),
            jax.ShapeDtypeStruct((scen, dates, own), F32),
            jax.ShapeDtypeStruct((dates, scen), F32),
            jax.ShapeDtypeStruct((dates, own), F32),
        ),
        in_specs=[hbm] * 8,
        out_specs=(vmem,) * 4,
        scratch_shapes=[
            pltpu.SMEM((dates, scen), F32),
            pltpu.SMEM((dates, scen), jnp.int32),
            pltpu.VMEM(by_year.shape, F32),
            pltpu.VMEM((years, cohorts), F32),
            pltpu.VMEM((1, cohorts), jnp.int32),
            pltpu.VMEM((scen, own), F32),
            pltpu.VMEM(weight.shape, BF16),
            pltpu.VMEM(growth.shape, F32),
            pltpu.VMEM((dates, rows, 4 * pad), BF16),
            pltpu.VMEM((terms, 4 * pad, lanes), BF16),
            pltpu.VMEM((terms, rows, lanes), F32),
            pltpu.VMEM((rows, lanes), F32),
            pltpu.VMEM((dates, rows, lanes), F32),
            pltpu.VMEM((scen, lanes), F32),
            pltpu.VMEM((rounds, scen, lanes), F32),
            pltpu.VMEM((rounds, n_in, scen, lanes), F32),
            pltpu.VMEM((scen, lanes), F32),
            pltpu.VMEM((dates, n_in, scen, 128), F32),
            pltpu.VMEM((dates, n_in, scen, 128), F32),
            pltpu.VMEM((8, lanes), F32),
            pltpu.VMEM((n_out, 8, lanes), F32),
            pltpu.SemaphoreType.DMA((8,)),
            pltpu.SemaphoreType.DMA((rounds, n_in)),
            pltpu.SemaphoreType.DMA((rounds, n_in)),
            pltpu.SemaphoreType.DMA((dates, n_in)),
            pltpu.SemaphoreType.DMA((dates, n_in)),
            pltpu.SemaphoreType.DMA((n_out,)),
            pltpu.SemaphoreType.DMA((n_out,)),
        ],
        compiler_params=pltpu.CompilerParams(
            collective_id=0, has_side_effects=True, vmem_limit_bytes=55168 * 1024
        ),
    )(node_rate.T, ladder_rung.T, by_year, cash_flows, owner_map.reshape(1, cohorts), capital, weight, growth)
    value, down, fund, summary = pl.pallas_call(
        deliver,
        out_shape=tuple(jax.ShapeDtypeStruct(x.shape, x.dtype) for x in results),
        in_specs=[pl.BlockSpec(memory_space=pl.ANY)] * 4,
        out_specs=(pl.BlockSpec(memory_space=pl.ANY),) * 4,
        scratch_shapes=[pltpu.SemaphoreType.DMA((4,))],
        compiler_params=pltpu.CompilerParams(vmem_limit_bytes=1024 * 1024),
    )(*results)
    return value, down, fund.T, summary


def deliver(*refs):
    count = (len(refs) - 1) // 2
    copies = [pltpu.make_async_copy(refs[i], refs[count + i], refs[-1].at[i]) for i in range(count)]
    for copy in copies:
        copy.start()
    for copy in copies:
        copy.wait()


def solution(mesh):
    return jax.shard_map(
        partial(shards, mesh.shape["inner"], mesh.shape["outer"]),
        mesh=mesh,
        in_specs=(
            P("outer", None, None, "inner"),
            P("outer", None),
            P("outer", None),
            P(),
            P(),
            P("outer", "inner"),
        ),
        out_specs=(
            P("outer", None, "inner"),
            P("outer", None, "inner"),
            P("outer", None),
            P(None, "inner"),
        ),
        check_vma=False,
    )
```
